32 devices in a mesh: groups: 2 (over y), fsdp: 8 (over z, x), dp: 1, sub: 2 (over core).
Axes of the slice: x: 2, y: 2, z: 4, core: 2. Of those that a mesh axis runs over, the one named last changes fastest.
Arguments:
- features: bfloat16 [16, 768, 1280], P(('groups', 'fsdp', 'dp'), 'sub'), parts along dimension 0, may hold values from -6 to 6
- golden: bfloat16 [4, 768, 1280], P(('groups', 'dp'), 'sub'), parts along dimension 0, may hold values from -6 to 6
- die_wafer: int32 [16], P(('groups', 'fsdp', 'dp')), parts along dimension 0, may hold values from 0 to 1
- norm_gain: float32 [1280], replicated, may hold values from 0.1 to 1.9
- proj_weight: bfloat16 [1280, 2560], P('fsdp'), may hold values from -0.15625 to 0.15625
- out_weight: bfloat16 [2560, 1280], P('fsdp'), may hold values from -0.125 to 0.125
- zero_weight: bfloat16 [1280, 1280], P(None, 'fsdp'), may hold values from -0.15625 to 0.15625
Outputs:
- block_out: bfloat16 [16, 768, 1280], P(('groups', 'fsdp', 'dp'), 'sub'), parts along dimension 0
The draws below stay inside these ranges and needn't reach their ends.
There are 2 independent parts, one for each index of `groups`. The reference program is written for one: setup_inputs(seed, part) draws one part's arguments, and reference() takes and returns one part's arrays. A program takes and returns all parts, laid end to end along the dimension named above; an argument that names none is the same for every part. Nothing has to cross between parts.
All inputs are finite; a program needn't handle non-finite values.
Results may differ from the reference program's by a relative error of at most 0.005.
Values may be sent and summed in bfloat16 or wider, within the bound.
A program may use at most 128 MiB of HBM per device.

```python
import jax
import jax.numpy as jnp
from jax import lax

C = 1280
FF = 2560
WAF = 2
POS = 768
DIES = 8
WAFERS = 2
N_DP = 1


def place_ends(result, rng, low, largest):
    longest = result.shape.index(max(result.shape))
    spots = []
    for shift in (0, 1):
        where = [jax.random.randint(jax.random.fold_in(rng, axis), (), 0, length) for axis, length in enumerate(result.shape)]
        where[longest] = (where[longest] + shift) % result.shape[longest]
        spots.append(tuple(where))
    return result.at[spots[0]].set(low).at[spots[1]].set(largest)


def levels(own_key, dims, shards, low, top_value):
    gain, own = 1.0, jax.random.fold_in(own_key, 6)
    for dim, blocks in shards:
        steps = jnp.exp(jax.random.uniform(jax.random.fold_in(own, dim), (blocks,), jnp.float32, low / len(shards), top_value / len(shards)))
        gain = gain * jnp.repeat(steps, dims[dim] // blocks).reshape([-1 if axis == dim else 1 for axis in range(len(dims))])
    return gain


def noise(stream_key, dims, spread, limit, shards=(), kind=jnp.bfloat16):
    loudness = levels(stream_key, dims, shards, -0.22, 0.18) if shards else 1.0
    array = jax.random.normal(stream_key, dims, jnp.float32) * spread * loudness
    return jnp.minimum(jnp.maximum(array, -limit), limit).astype(kind)


def setup_inputs(seed: int = 0, part: int = 0) -> dict:
    key_of = jax.random.split(jax.random.key(seed), 8)
    part_splits = jax.random.split(jax.random.fold_in(key_of[7], part), 8)
    features = noise(part_splits[0], (DIES, POS, C), 1.0, 6.0, ((0, 8), (1, 2)))
    golden = noise(part_splits[1], (WAFERS, POS, C), 1.0, 6.0, ((1, 2),))
    die_wafer = place_ends(jax.random.randint(part_splits[2], (DIES,), 0, WAF), jax.random.fold_in(part_splits[2], 1), 0, WAF - 1).astype(jnp.int32)
    norm_gain = jnp.clip(1.0 + 0.18 * jax.random.normal(key_of[3], (C,), jnp.float32), 0.1, 1.9)
    proj_weight = noise(key_of[4], (C, FF), C ** -0.5, 0.15625, ((0, 8),))
    out_weight = noise(key_of[5], (FF, C), FF ** -0.5, 0.125, ((0, 8),))
    zero_weight = noise(key_of[6], (C, C), C ** -0.5, 0.15625, ((1, 8),))
    return {"features": features, "golden": golden, "die_wafer": die_wafer, "norm_gain": norm_gain, "proj_weight": proj_weight, "out_weight": out_weight, "zero_weight": zero_weight}


def reference(features, golden, die_wafer, norm_gain, proj_weight, out_weight, zero_weight):

    def zero_conv(golden_one):
        return jnp.dot(golden_one, zero_weight, preferred_element_type=jnp.float32).astype(jnp.bfloat16)
    control = lax.map(zero_conv, golden)
    die_index = jnp.arange(DIES, dtype=jnp.int32)
    wafer_index = (die_index % N_DP * WAF + die_wafer).astype(jnp.int32)

    def one_die(operands):
        feature_one, wafer_one = operands
        residual = lax.dynamic_index_in_dim(control, wafer_one, 0, keepdims=False)
        mixed = feature_one.astype(jnp.float32) + residual.astype(jnp.float32)
        average = lax.optimization_barrier(jnp.mean(mixed, axis=-1, keepdims=True))
        centred = mixed - average
        variance = lax.optimization_barrier(jnp.mean(centred * centred, axis=-1, keepdims=True))
        normed = (centred * lax.rsqrt(variance + 1e-05) * norm_gain).astype(jnp.bfloat16)
        preact = jnp.dot(normed, proj_weight, preferred_element_type=jnp.float32)
        hidden = jax.nn.gelu(preact, approximate=True).astype(jnp.bfloat16)
        branch = jnp.dot(hidden, out_weight, preferred_element_type=jnp.float32)
        return (mixed + branch).astype(jnp.bfloat16)
    return lax.map(one_die, (features, wafer_index))
```

```python
import functools

import jax
import jax.numpy as jnp
from jax import lax
from jax.experimental import pallas as pl
from jax.experimental.pallas import tpu as pltpu
from jax.sharding import PartitionSpec as P

MESH = pl.DeviceIdType.MESH
TILE = 256


def kernel(n, snake, die_ref, gain_ref, feat_hbm, gold_hbm, z_hbm, p_hbm, o_hbm, out_ref,
           feat, gold, zb, pb, ob, mixed, normed, hidden,
           ring_send, ring_recv, y_send, y_recv, sib_send, sib_recv, local_sem):
    y = lax.axis_index("groups")
    me = lax.axis_index("fsdp")
    core = lax.axis_index("sub")
    steps = n - 1
    rows, width = feat.shape
    ff = hidden.shape[1]
    rp = z_hbm.shape[0]
    ro = o_hbm.shape[0]

    def place_of(idx):
        if not snake:
            return idx
        half, odd = lax.div(idx, 2), lax.rem(idx, 2)
        return half * (1 - odd) + odd * (n - 1 - half)

    def index_at(place):
        if not snake:
            return place
        back = lax.div(place, n // 2)
        return (1 - back) * 2 * place + back * (2 * (n - 1 - place) + 1)

    here = place_of(me)

    def at(shift):
        return index_at(lax.rem(here + shift + 2 * n, n))

    ahead, behind = {"fsdp": at(1)}, {"fsdp": at(-1)}
    across, sibling = {"groups": 1 - y}, {"sub": 1 - core}

    locals_ = [
        pltpu.make_async_copy(p_hbm, pb.at[pl.ds(pl.multiple_of(me * rp, 16), rp), :], local_sem.at[0]),
        pltpu.make_async_copy(z_hbm, zb.at[pl.ds(pl.multiple_of(me * rp, 16), rp), :], local_sem.at[1]),
        pltpu.make_async_copy(o_hbm, ob.at[pl.ds(pl.multiple_of(me * ro, 16), ro), :], local_sem.at[2]),
        pltpu.make_async_copy(gold_hbm, gold, local_sem.at[3]),
        pltpu.make_async_copy(feat_hbm, feat, local_sem.at[4]),
    ]
    for copy in locals_:
        copy.start()

    barrier = pltpu.get_barrier_semaphore()
    for other in (ahead, behind, across, sibling):
        pl.semaphore_signal(barrier, inc=1, device_id=other, device_id_type=MESH)
    for copy in locals_[:3]:
        copy.wait()
    pl.semaphore_wait(barrier, 4)

    first = (width // TILE + 1) // 2 * TILE
    half = width // 2
    ru = rp // 16
    qu = ro // 2 // 16
    streams = [
        (zb, rp, 0, rp, 0, half, half, ru // 3 * 16),
        (pb, rp, 0, rp, 0, ff // 4, ff // 4, ru // 3 * 16),
        (pb, rp, 0, rp, ff // 2, ff // 4, ff // 4, ru // 3 * 16),
        (ob, ro, ro // 2, ro // 2, 0, 0, first, (qu + 2) // 3 * 16),
        (ob, ro, ro // 2, ro // 2, first, 0, width - first, (qu + 2) // 3 * 16),
    ]

    def piece(j, owner, part, who):
        buf, per, core_rows, count, col, core_cols, cols, outer = streams[j]
        row = owner * per + who * core_rows
        if part == 0:
            row, size = row + y * (count - outer), outer
        elif part == 1:
            row, size = row + outer, count - 2 * outer
        else:
            row, size = row + (1 - y) * (count - outer), outer
        start = col + who * core_cols if core_cols else col
        if core_cols:
            start = pl.multiple_of(start, 128)
        return buf.at[pl.ds(pl.multiple_of(row, 16), size), pl.ds(start, cols)]

    pending = []

    def remote(ref, send, recv, to):
        return pltpu.make_async_remote_copy(
            src_ref=ref, dst_ref=ref, send_sem=send, recv_sem=recv, device_id=to, device_id_type=MESH)

    def send(ref, s, r, to):
        copy = remote(ref, s, r, to)
        copy.start()
        pending.append(copy)

    def came(ref, s, r, to):
        remote(ref, s, r, to).wait_recv()

    def to_sibling(j, t, part, owner):
        send(piece(j, owner, part, core), sib_send.at[j, t, part], sib_recv.at[j, t, part], sibling)

    def event(j, s):
        if s == 0:
            send(piece(j, me, 0, core), ring_send.at[j, 0, 0], ring_recv.at[j, 0, 0], ahead)
            send(piece(j, me, 1, core), ring_send.at[j, 0, 1], ring_recv.at[j, 0, 1], behind)
            return
        t = s - 1
        if t < steps:
            owner = at(-1 - t)
            ref = piece(j, owner, 0, core)
            came(ref, ring_send.at[j, t, 0], ring_recv.at[j, t, 0], ahead)
            if s < steps:
                send(ref, ring_send.at[j, s, 0], ring_recv.at[j, s, 0], ahead)
            send(ref, y_send.at[j, t], y_recv.at[j, t], across)
            to_sibling(j, t, 0, owner)
            owner = at(1 + t)
            ref = piece(j, owner, 1, core)
            came(ref, ring_send.at[j, t, 1], ring_recv.at[j, t, 1], behind)
            if s < steps:
                send(ref, ring_send.at[j, s, 1], ring_recv.at[j, s, 1], behind)
            to_sibling(j, t, 1, owner)
        if t >= 1:
            owner = at(-t)
            came(piece(j, owner, 2, core), y_send.at[j, t - 1], y_recv.at[j, t - 1], across)
            to_sibling(j, t - 1, 2, owner)

    def arrived(j):
        for t in range(steps):
            for part, owner in ((0, at(-1 - t)), (1, at(1 + t)), (2, at(-1 - t))):
                came(piece(j, owner, part, 1 - core), sib_send.at[j, t, part], sib_recv.at[j, t, part], sibling)

    wafer = die_ref[0]

    def control():
        arrived(0)
        locals_[3].wait()
        locals_[4].wait()

        @pl.loop(0, width // TILE)
        def _(i):
            cols = pl.ds(pl.multiple_of(i * TILE, TILE), TILE)
            residual = lax.dot_general(
                gold[wafer], zb[cols, :], (((1,), (1,)), ((), ())), preferred_element_type=jnp.float32
            ).astype(jnp.bfloat16)
            mixed[:, cols] = feat[:, cols].astype(jnp.float32) + residual.astype(jnp.float32)

    def norm():
        gain = gain_ref[...]

        @pl.loop(0, rows // 32)
        def _(i):
            part = pl.ds(pl.multiple_of(i * 32, 32), 32)
            value = mixed[part, :]
            centred = value - jnp.mean(value, axis=-1, keepdims=True)
            variance = jnp.mean(centred * centred, axis=-1, keepdims=True)
            normed[part, :] = (centred * lax.rsqrt(variance + 1e-05) * gain).astype(jnp.bfloat16)

    def project(low, high):
        @pl.loop(low // TILE, high // TILE)
        def _(i):
            cols = pl.ds(pl.multiple_of(i * TILE, TILE), TILE)
            preact = jnp.dot(normed[...], pb[:, cols], preferred_element_type=jnp.float32)
            hidden[:, cols] = jax.nn.gelu(preact, approximate=True).astype(jnp.bfloat16)

    def output(low, high):
        @pl.loop(low // TILE, high // TILE)
        def _(i):
            cols = pl.ds(pl.multiple_of(i * TILE, TILE), TILE)
            branch = jnp.dot(hidden[...], ob[:, cols], preferred_element_type=jnp.float32)
            out_ref[:, cols] = (mixed[:, cols] + branch).astype(jnp.bfloat16)

    scale = steps / 7
    starts = (0.0, 0.5, 14.0 * scale, 14.3 * scale, 14.6 * scale)
    paces = (2.0, 2.0, 2.2, 2.7, 3.0)
    plan = [(starts[j] + paces[j] * s, j, functools.partial(event, j, s)) for j in range(5) for s in range(n + 1)]

    def end(j):
        return starts[j] + paces[j] * n

    plan += [
        (end(0) + 2.1, 9, control),
        (end(0) + 3.1, 9, norm),
        (end(1) + 4.1, 9, lambda: (arrived(1), project(0, ff // 4 // TILE * TILE))),
        (end(1) + 6.1, 9, lambda: project(ff // 4 // TILE * TILE, ff // 2)),
        (end(2) + 2.1, 9, lambda: (arrived(2), project(ff // 2, ff // 2 + ff // 4 // TILE * TILE))),
        (end(2) + 3.1, 9, lambda: project(ff // 2 + ff // 4 // TILE * TILE, ff)),
        (end(3) + 2.1, 9, lambda: (arrived(3), output(0, first))),
        (end(4) + 9.1, 9, lambda: (arrived(4), output(first, width))),
    ]
    for _, _, act in sorted(plan, key=lambda item: item[:2]):
        act()
    for copy in pending:
        copy.wait_send()


def body(n, snake, features, golden, die_wafer, norm_gain, proj_weight, out_weight, zero_weight):
    rows, width = features.shape[1:]
    ff = proj_weight.shape[1]
    dma = pltpu.SemaphoreType.DMA
    anywhere = pl.BlockSpec(memory_space=pl.ANY)
    out = pl.pallas_call(
        functools.partial(kernel, n, snake),
        out_shape=jax.ShapeDtypeStruct((rows, width), jnp.bfloat16),
        in_specs=[pl.BlockSpec(memory_space=pltpu.SMEM), pl.BlockSpec(memory_space=pltpu.VMEM)] + [anywhere] * 5,
        out_specs=pl.BlockSpec(memory_space=pltpu.VMEM),
        scratch_shapes=[
            pltpu.VMEM((rows, width), jnp.bfloat16),
            pltpu.VMEM(golden.shape, jnp.bfloat16),
            pltpu.VMEM((width, width), jnp.bfloat16),
            pltpu.VMEM((width, ff), jnp.bfloat16),
            pltpu.VMEM((ff, width), jnp.bfloat16),
            pltpu.VMEM((rows, width), jnp.float32),
            pltpu.VMEM((rows, width), jnp.bfloat16),
            pltpu.VMEM((rows, ff), jnp.bfloat16),
            dma((5, n - 1, 2)), dma((5, n - 1, 2)),
            dma((5, n - 1)), dma((5, n - 1)),
            dma((5, n - 1, 3)), dma((5, n - 1, 3)),
            dma((5,)),
        ],
        compiler_params=pltpu.CompilerParams(
            collective_id=0, has_side_effects=True, vmem_limit_bytes=48 * 1024 * 1024),
    )(die_wafer, norm_gain[None], features[0], golden, zero_weight.T, proj_weight, out_weight)
    return out[None]


def solution(mesh):
    placed = (
        P(("groups", "fsdp", "dp"), "sub", None),
        P(("groups", "dp"), "sub", None),
        P(("groups", "fsdp", "dp")),
        P(),
        P("fsdp", None),
        P("fsdp", None),
        P(None, "fsdp"),
    )
    return jax.shard_map(
        functools.partial(body, mesh.shape["fsdp"], mesh.shape["dp"] == 1),
        mesh=mesh,
        in_specs=placed,
        out_specs=P(("groups", "fsdp", "dp"), "sub", None),
        check_vma=False,
    )
```

```python
import functools

import jax
import jax.numpy as jnp
from jax import lax
from jax.experimental import pallas as pl
from jax.experimental.pallas import tpu as pltpu
from jax.sharding import PartitionSpec as P

MESH = pl.DeviceIdType.MESH
TILE = 256
STREAMS = (("z", 0, 5), ("p", 0, 5), ("p", 5, 10), ("o", 0, 3), ("o", 3, 5))
STARTS = (0, 0.2, 0.4, 6.0, 7.0)
PACES = (3.0, 3.6, 4.2, 4.1, 4.1)
DELAYS = (2.0, 2.0, 2.0, 2.0, 9.0)
GROUP = 1
GAP = 1.0


def kernel(n, snake, die_ref, gain_ref, feat_hbm, gold_hbm, z_hbm, p_hbm, o_hbm, out_ref,
           feat, gold, zb, pb, ob, mixed, normed, hidden,
           ring_send, ring_recv, y_send, y_recv, sib_send, sib_recv, local_sem):
    y = lax.axis_index("groups")
    me = lax.axis_index("fsdp")
    core = lax.axis_index("sub")
    steps = n - 1
    rows, width = feat.shape
    ff = hidden.shape[1]
    rp = z_hbm.shape[0]
    ro = o_hbm.shape[0]

    def place_of(idx):
        if not snake:
            return idx
        half, odd = lax.div(idx, 2), lax.rem(idx, 2)
        return half * (1 - odd) + odd * (n - 1 - half)

    def index_at(place):
        if not snake:
            return place
        back = lax.div(place, n // 2)
        return (1 - back) * 2 * place + back * (2 * (n - 1 - place) + 1)

    here = place_of(me)

    around = {}

    def at(shift):
        shift %= n
        if shift not in around:
            around[shift] = index_at(lax.rem(here + shift, n))
        return around[shift]

    ahead, behind = {"fsdp": at(1)}, {"fsdp": at(-1)}
    across, sibling = {"groups": 1 - y}, {"sub": 1 - core}

    locals_ = [
        pltpu.make_async_copy(p_hbm, pb.at[pl.ds(pl.multiple_of(me * rp, 16), rp), :], local_sem.at[0]),
        pltpu.make_async_copy(z_hbm, zb.at[pl.ds(pl.multiple_of(me * rp, 16), rp), :], local_sem.at[1]),
        pltpu.make_async_copy(o_hbm, ob.at[pl.ds(pl.multiple_of(me * ro, 16), ro), :], local_sem.at[2]),
        pltpu.make_async_copy(gold_hbm, gold, local_sem.at[3]),
        pltpu.make_async_copy(feat_hbm, feat, local_sem.at[4]),
    ]
    for copy in locals_:
        copy.start()

    barrier = pltpu.get_barrier_semaphore()
    for other in (ahead, behind, across, sibling):
        pl.semaphore_signal(barrier, inc=1, device_id=other, device_id_type=MESH)
    for copy in locals_[:3]:
        copy.wait()
    pl.semaphore_wait(barrier, 4)

    ru = rp // 16
    qu = ro // 2 // 16

    def stream(kind, low, high):
        low, high = low * TILE, high * TILE
        if kind == "o":
            return ob, ro, ro // 2, ro // 2, low, 0, high - low, (qu + 2) // 3 * 16
        half = (high - low) // 2
        return {"z": zb, "p": pb}[kind], rp, 0, rp, low, half, half, ru // 3 * 16

    streams = [stream(*item) for item in STREAMS]

    def piece(j, owner, part, who):
        buf, per, core_rows, count, col, core_cols, cols, outer = streams[j]
        row = owner * per + who * core_rows
        if part == 0:
            row, size = row + y * (count - outer), outer
        elif part == 1:
            row, size = row + outer, count - 2 * outer
        else:
            row, size = row + (1 - y) * (count - outer), outer
        start = col + who * core_cols if core_cols else col
        if core_cols:
            start = pl.multiple_of(start, 128)
        return buf.at[pl.ds(pl.multiple_of(row, 16), size), pl.ds(start, cols)]

    pending = []

    def remote(ref, send, recv, to):
        return pltpu.make_async_remote_copy(
            src_ref=ref, dst_ref=ref, send_sem=send, recv_sem=recv, device_id=to, device_id_type=MESH)

    def send(ref, s, r, to):
        copy = remote(ref, s, r, to)
        copy.start()
        pending.append(copy)

    def came(ref, s, r, to):
        remote(ref, s, r, to).wait_recv()

    def to_sibling(j, t, part, owner):
        send(piece(j, owner, part, core), sib_send.at[j, t, part], sib_recv.at[j, t, part], sibling)

    def event(j, s):
        if s == 0:
            send(piece(j, me, 0, core), ring_send.at[j, 0, 0], ring_recv.at[j, 0, 0], ahead)
            send(piece(j, me, 1, core), ring_send.at[j, 0, 1], ring_recv.at[j, 0, 1], behind)
            return
        t = s - 1
        if t < steps:
            owner = at(-1 - t)
            ref = piece(j, owner, 0, core)
            came(ref, ring_send.at[j, t, 0], ring_recv.at[j, t, 0], ahead)
            if s < steps:
                send(ref, ring_send.at[j, s, 0], ring_recv.at[j, s, 0], ahead)
            send(ref, y_send.at[j, t], y_recv.at[j, t], across)
            to_sibling(j, t, 0, owner)
            owner = at(1 + t)
            ref = piece(j, owner, 1, core)
            came(ref, ring_send.at[j, t, 1], ring_recv.at[j, t, 1], behind)
            if s < steps:
                send(ref, ring_send.at[j, s, 1], ring_recv.at[j, s, 1], behind)
            to_sibling(j, t, 1, owner)
        if t >= 1:
            owner = at(-t)
            came(piece(j, owner, 2, core), y_send.at[j, t - 1], y_recv.at[j, t - 1], across)
            to_sibling(j, t - 1, 2, owner)

    def arrived(j):
        for t in range(steps):
            for part, owner in ((0, at(-1 - t)), (1, at(1 + t)), (2, at(-1 - t))):
                came(piece(j, owner, part, 1 - core), sib_send.at[j, t, part], sib_recv.at[j, t, part], sibling)

    wafer = die_ref[0]

    def tiles(low, high, step):
        def loop():
            @pl.loop(low, high)
            def _(i):
                step(pl.ds(pl.multiple_of(i * TILE, TILE), TILE))
        return loop

    def control(cols):
        residual = lax.dot_general(
            gold[wafer], zb[cols, :], (((1,), (1,)), ((), ())), preferred_element_type=jnp.float32
        ).astype(jnp.bfloat16)
        mixed[:, cols] = feat[:, cols].astype(jnp.float32) + residual.astype(jnp.float32)

    def norm():
        gain = gain_ref[...][None]

        @pl.loop(0, rows // 32)
        def _(i):
            part = pl.ds(pl.multiple_of(i * 32, 32), 32)
            value = mixed[part, :]
            centred = value - jnp.mean(value, axis=-1, keepdims=True)
            variance = jnp.mean(centred * centred, axis=-1, keepdims=True)
            normed[part, :] = (centred * lax.rsqrt(variance + 1e-05) * gain).astype(jnp.bfloat16)

    def project(cols):
        preact = jnp.dot(normed[...], pb[:, cols], preferred_element_type=jnp.float32)
        hidden[:, cols] = jax.nn.gelu(preact, approximate=True).astype(jnp.bfloat16)

    def output(cols):
        branch = jnp.dot(hidden[...], ob[:, cols], preferred_element_type=jnp.float32)
        out_ref[:, cols] = (mixed[:, cols] + branch).astype(jnp.bfloat16)

    scale = steps / 7
    count = len(STREAMS)
    plan = [(STARTS[j] * scale + PACES[j] * s, j, functools.partial(event, j, s)) for j in range(count) for s in range(n + 1)]
    clock = 0.0
    for j, (kind, low, high) in enumerate(STREAMS):
        clock = max(clock, STARTS[j] * scale + PACES[j] * n + DELAYS[j])
        acts = [functools.partial(arrived, j)]
        if j == 0:
            acts += [locals_[3].wait, locals_[4].wait]
        step = {"z": control, "p": project, "o": output}[kind]
        acts += [tiles(i, min(i + GROUP, high), step) for i in range(low, high, GROUP)]
        if kind == "z":
            acts.append(norm)
        for act in acts:
            plan.append((clock, 99, act))
            if act not in acts[:1]:
                clock += GAP
    for _, _, act in sorted(plan, key=lambda item: item[:2]):
        act()
    for copy in pending:
        copy.wait_send()


def body(n, snake, features, golden, die_wafer, norm_gain, proj_weight, out_weight, zero_weight):
    rows, width = features.shape[1:]
    ff = proj_weight.shape[1]
    dma = pltpu.SemaphoreType.DMA
    count = len(STREAMS)
    anywhere = pl.BlockSpec(memory_space=pltpu.HBM)
    out = pl.pallas_call(
        functools.partial(kernel, n, snake),
        out_shape=jax.ShapeDtypeStruct((rows, width), jnp.bfloat16),
        in_specs=[pl.BlockSpec(memory_space=pltpu.SMEM), pl.BlockSpec(memory_space=pltpu.VMEM)] + [anywhere] * 5,
        out_specs=pl.BlockSpec(memory_space=pltpu.VMEM),
        scratch_shapes=[
            pltpu.VMEM((rows, width), jnp.bfloat16),
            pltpu.VMEM(golden.shape, jnp.bfloat16),
            pltpu.VMEM((width, width), jnp.bfloat16),
            pltpu.VMEM((width, ff), jnp.bfloat16),
            pltpu.VMEM((ff, width), jnp.bfloat16),
            pltpu.VMEM((rows, width), jnp.float32),
            pltpu.VMEM((rows, width), jnp.bfloat16),
            pltpu.VMEM((rows, ff), jnp.bfloat16),
            dma((count, n - 1, 2)), dma((count, n - 1, 2)),
            dma((count, n - 1)), dma((count, n - 1)),
            dma((count, n - 1, 3)), dma((count, n - 1, 3)),
            dma((5,)),
        ],
        compiler_params=pltpu.CompilerParams(
            collective_id=0, has_side_effects=True, vmem_limit_bytes=48 * 1024 * 1024),
    )(die_wafer, norm_gain, features[0], golden, zero_weight.T, proj_weight, out_weight)
    return out[None]


def solution(mesh):
    placed = (
        P(("groups", "fsdp", "dp"), "sub", None),
        P(("groups", "dp"), "sub", None),
        P(("groups", "fsdp", "dp")),
        P(),
        P("fsdp", None),
        P("fsdp", None),
        P(None, "fsdp"),
    )
    return jax.shard_map(
        functools.partial(body, mesh.shape["fsdp"], mesh.shape["dp"] == 1),
        mesh=mesh,
        in_specs=placed,
        out_specs=P(("groups", "fsdp", "dp"), "sub", None),
        check_vma=False,
    )
```
